32 devices in a mesh: groups: 2 (over x), ent: 16 (over z, y, core).
Axes of the slice: x: 2, y: 2, z: 4, core: 2. Of those that a mesh axis runs over, the one named last changes fastest.
Arguments:
- entity: float32 [32768, 400], P(('groups', 'ent')), parts along dimension 0, may hold values from -4 to 4
- entity_state: float32 [32768], P(('groups', 'ent')), parts along dimension 0, may hold values from 0.01 to 1
- relation: float32 [4352, 400], P('groups'), parts along dimension 0, may hold values from 0.5 to 1.5
- relation_state: float32 [4352], P('groups'), parts along dimension 0, may hold values from 0.01 to 1
- src_offset: int32 [32768], P(('groups', 'ent')), parts along dimension 0, may hold values from 0 to 1023
- dst_part: int32 [32768, 1], P(('groups', 'ent')), parts along dimension 0, may hold values from 0 to 15; in each aligned block of 1024 rows (0 to 1023, 1024 to 2047, ...) at most 128 rows name the same one
- dst_offset: int32 [32768], P(('groups', 'ent')), parts along dimension 0, may hold values from 0 to 1023
- rel_id: int32 [32768], P(('groups', 'ent')), parts along dimension 0, may hold values from 0 to 2175
Outputs:
- new_entity: float32 [32768, 400], P(('groups', 'ent')), parts along dimension 0
- new_entity_state: float32 [32768], P(('groups', 'ent')), parts along dimension 0
- new_relation: float32 [4352, 400], P('groups'), parts along dimension 0
- new_relation_state: float32 [4352], P('groups'), parts along dimension 0
- edge_loss: float32 [32768], P(('groups', 'ent')), parts along dimension 0
The draws below stay inside these ranges and needn't reach their ends.
There are 2 independent parts, one for each index of `groups`. The reference program is written for one: setup_inputs(seed, part) draws one part's arguments, and reference() takes and returns one part's arrays. A program takes and returns all parts, laid end to end along the dimension named above; each array names one. Nothing has to cross between parts.
Inputs may be any that keep to these rules, and one draw needn't show every extreme that they name: `dst_part`: at most 128 of the edges held by one partition have one destination partition, and in every draw some partition has exactly 128 edges for one destination partition.
All inputs are finite; a program needn't handle non-finite values.
Results may differ from the reference program's by a relative error of at most 0.0024.
Values may be sent and summed in bfloat16 or wider, within the bound.
A program may use at most 128 MiB of HBM per device.

```python
import math
import jax
import jax.numpy as jnp
import numpy as np
from jax import lax

D = 400
NREL = 2176
ROWS_DEV = 1024
EDGE_DEV = 1024
BLOCK = 1024
CAP = 128
ENTS = 16384
EDGES = 16384
N_ENT = 16


def draw_entity(key, part):
    key = jax.random.fold_in(key, 11)
    key_base = jax.random.fold_in(key, 0)
    values = 0.25 * jax.random.normal(key_base, (ENTS, D), jnp.float32)
    return jnp.clip(values, -4.0, 4.0)


def place_ends(entries, key, smallest, largest):
    longest = entries.shape.index(max(entries.shape))
    spots = []
    for shift in (0, 1):
        where = [jax.random.randint(jax.random.fold_in(key, axis), (), 0, length) for axis, length in enumerate(entries.shape)]
        where[longest] = (where[longest] + shift) % entries.shape[longest]
        spots.append(tuple(where))
    return entries.at[spots[0]].set(smallest).at[spots[1]].set(largest)


def block_scale(key, dims, cuts, low, largest):
    level, own = 1.0, jax.random.fold_in(key, 6)
    for position, shards_of in cuts:
        draws = jnp.exp(jax.random.uniform(jax.random.fold_in(own, position), (shards_of,), jnp.float32, low / len(cuts), largest / len(cuts)))
        level = level * jnp.repeat(draws, dims[position] // shards_of).reshape([-1 if axis == position else 1 for axis in range(len(dims))])
    return level


def shared_out(stream_key, own, number, rows, count, top, limit, skew):
    ranking = jax.random.permutation(stream_key, count)
    crowded, usual = portions_of(count, rows * top, limit, skew, True), portions_of(count, rows * top, limit, skew, False)
    places = jnp.arange(count)

    def named(tallies, offset_by):
        used = int((tallies > 0).sum())
        fixed = max(1, used // 4)
        passed = fixed + (places - fixed + offset_by * (used - fixed)) % max(1, count - fixed)
        return jnp.zeros((count,), jnp.int32).at[ranking[jnp.where(places < fixed, places, passed)]].set(jnp.asarray(tallies, jnp.int32))

    tallies = jnp.where(number % 4 == 0, named(crowded, number // 4), named(usual, number - number // 4 - 1))
    mixed = jax.random.permutation(jax.random.fold_in(own, 3), count)
    giver, taker = mixed[0:count // 2 * 2:2], mixed[1:count // 2 * 2:2]
    margin = jnp.minimum(tallies[giver] - 1, limit - tallies[taker]) // 2
    margin = jnp.where((giver == ranking[0]) | (taker == ranking[0]) | (tallies[taker] == 0), 0, jnp.maximum(margin, 0))
    passed = jax.random.randint(jax.random.fold_in(own, 4), (count // 2,), 0, 1 << 20) % (margin + 1)
    tallies = tallies.at[giver].add(-passed).at[taker].add(passed)
    members = jnp.searchsorted(jnp.cumsum(tallies), jnp.arange(rows * top), side="right").astype(jnp.int32)
    grid = members.reshape(top, rows).T
    grid = grid[jax.random.permutation(jax.random.fold_in(own, 1), rows)]
    offset_by = jax.random.randint(jax.random.fold_in(own, 2), (rows, 1), 0, top)
    return jnp.take_along_axis(grid, (jnp.arange(top)[None, :] + offset_by) % top, axis=1)


def portions_of(count, total, limit, lean, full):
    weights = [(1 << 20) // math.isqrt(rank ** lean) + 1 for rank in range(1, count + 1)]
    largest = limit if full else min(limit, max(-(-total // count), total * weights[0] // sum(weights)))
    least = 1 if total - largest >= count - 1 else 0
    counts, rest = [largest] + [least] * (count - 1), total - largest - least * (count - 1)
    while rest > 0:
        candidates = [i for i in range(1, count) if counts[i] < largest] or [i for i in range(1, count) if counts[i] < limit]
        pool, remaining = sum([weights[i] for i in candidates]), rest
        for i in candidates:
            more = min(limit - counts[i], max(1, remaining * weights[i] // pool), rest)
            counts[i] = counts[i] + more
            rest = rest - more
    return np.array(counts)


def setup_inputs(seed: int = 0, part: int = 0) -> dict:
    splits = jax.random.split(jax.random.key(seed), 9)
    part_splits = jax.random.split(jax.random.fold_in(splits[8], part), 9)
    entity = draw_entity(jax.random.fold_in(jax.random.fold_in(splits[8], part), 71), part)
    entity_state = jnp.clip(jnp.exp(math.log(1.0) - 4.6051702 * jax.random.uniform(part_splits[1], (ENTS,), jnp.float32) ** block_scale(part_splits[1], (ENTS,), ((0, 16),), -0.2, 0.2)), 0.01, 1.0)
    relation = jnp.clip(jax.random.uniform(part_splits[2], (NREL, D), jnp.float32, 0.5, 1.5), 0.5, 1.5)
    relation_state = jnp.clip(jnp.exp(jax.random.uniform(part_splits[3], (NREL,), jnp.float32, math.log(0.01), math.log(1.0))), 0.01, 1.0)
    src_offset = place_ends(jax.random.randint(part_splits[4], (EDGES,), 0, ROWS_DEV), jax.random.fold_in(part_splits[4], 1), 0, ROWS_DEV - 1).astype(jnp.int32)
    dst_part_keys = jax.random.split(jax.random.fold_in(part_splits[5], 1), EDGES // EDGE_DEV)
    dst_part_turns = jax.random.permutation(jax.random.fold_in(part_splits[5], 3), EDGES // EDGE_DEV)
    dst_part = jax.vmap(lambda own, number: shared_out(jax.random.fold_in(part_splits[5], 2), own, number, EDGE_DEV, N_ENT, 1, CAP, 1))(dst_part_keys, dst_part_turns).reshape((EDGES, 1))
    dst_offset = place_ends(jax.random.randint(part_splits[6], (EDGES,), 0, ROWS_DEV), jax.random.fold_in(part_splits[6], 1), 0, ROWS_DEV - 1).astype(jnp.int32)
    rel_id = place_ends(jax.random.randint(part_splits[7], (EDGES,), 0, NREL), jax.random.fold_in(part_splits[7], 1), 0, NREL - 1).astype(jnp.int32)
    return dict(entity=entity, entity_state=entity_state, relation=relation, relation_state=relation_state, src_offset=src_offset, dst_part=dst_part, dst_offset=dst_offset, rel_id=rel_id)


learn_rate = 0.3

def score_block(pair):
    queries, targets = pair
    query_full = queries.astype(jnp.float32)
    target_full = targets.astype(jnp.float32)
    logits = jnp.dot(query_full, target_full.T, preferred_element_type=jnp.float32)
    row_max = lax.optimization_barrier(jnp.max(logits, axis=1, keepdims=True))
    log_total = jnp.log(lax.optimization_barrier(jnp.sum(jnp.exp(logits - row_max), axis=1, keepdims=True))) + row_max
    softmax_w = jnp.exp(logits - log_total)
    identity = jnp.eye(BLOCK, dtype=jnp.float32)
    edge_loss = log_total[:, 0] - lax.optimization_barrier(jnp.sum(logits * identity, axis=1))
    coefficient = (softmax_w - identity).astype(jnp.bfloat16).astype(jnp.float32)
    query_grad = jnp.dot(coefficient, target_full, preferred_element_type=jnp.float32)
    target_grad = jnp.dot(coefficient.T, query_full, preferred_element_type=jnp.float32)
    return (edge_loss, query_grad, target_grad)

def reference(entity, entity_state, relation, relation_state, src_offset, dst_part, dst_offset, rel_id):
    holder = jnp.arange(EDGES, dtype=jnp.int32) // EDGE_DEV
    src_row = (holder * ROWS_DEV + src_offset).astype(jnp.int32)
    dst_row = (dst_part[:, 0] * ROWS_DEV + dst_offset).astype(jnp.int32)
    sources = entity[src_row]
    weights = relation[rel_id]
    queries = (sources * weights).astype(jnp.bfloat16)
    targets = entity[dst_row].astype(jnp.bfloat16)
    block_count = EDGES // BLOCK
    edge_loss, query_grad, target_grad = lax.map(score_block, (queries.reshape(block_count, BLOCK, D), targets.reshape(block_count, BLOCK, D)))
    edge_loss = edge_loss.reshape(EDGES)
    query_grad = query_grad.reshape(EDGES, D)
    target_grad = target_grad.reshape(EDGES, D)
    entity_grad = jnp.zeros((ENTS, D), jnp.float32)
    entity_grad = entity_grad.at[src_row].add(query_grad * weights)
    entity_grad = entity_grad.at[dst_row].add(target_grad)
    relation_grad = jnp.zeros((NREL, D), jnp.float32).at[rel_id].add(query_grad * sources)
    new_entity_state = entity_state + lax.optimization_barrier(jnp.mean(entity_grad * entity_grad, axis=1))
    new_entity = entity - learn_rate * entity_grad / jnp.sqrt(new_entity_state)[:, None]
    new_relation_state = relation_state + lax.optimization_barrier(jnp.mean(relation_grad * relation_grad, axis=1))
    new_relation = relation - learn_rate * relation_grad / jnp.sqrt(new_relation_state)[:, None]
    return (new_entity, new_entity_state, new_relation, new_relation_state, edge_loss)
```

```python
import functools

import jax
import jax.numpy as jnp
from jax import lax
from jax.experimental import pallas as pl
from jax.experimental.pallas import tpu as pltpu
from jax.sharding import PartitionSpec as P

BLOCK = 1024
TILE = 256
learn_rate = 0.3

f32, bf16, i32 = jnp.float32, jnp.bfloat16, jnp.int32
VM = pltpu.VMEM


def nt(a, b):
    return lax.dot_general(a, b, (((1,), (1,)), ((), ())), preferred_element_type=f32)


def tn(a, b):
    return lax.dot_general(a, b, (((0,), (0,)), ((), ())), preferred_element_type=f32)


def nn(a, b):
    return jnp.dot(a, b, preferred_element_type=f32)


def hits(first, count, row):
    return lax.broadcasted_iota(i32, (count, row.shape[1]), 0) + first == row


def ones_at(first, count, row):
    return jnp.where(hits(first, count, row), 1.0, 0.0).astype(bf16)


def tiles(total, body, size=TILE):
    whole = total // size

    def step(t, carry):
        body(pl.multiple_of(t * size, size), size)
        return carry

    lax.fori_loop(0, whole, step, 0)
    if total % size:
        body(whole * size, total % size)


def split3(x):
    high = x.astype(bf16)
    rest = x - high.astype(f32)
    mid = rest.astype(bf16)
    return high, mid, (rest - mid.astype(f32)).astype(bf16)


def rank_kernel(owners, cap, part_ref, off_ref, slot_ref, req_ref):
    part, off = part_ref[...], off_ref[...]
    edges = part.shape[1]
    mine = hits(0, owners, part)
    earlier = lax.broadcasted_iota(i32, (edges, edges), 0) < lax.broadcasted_iota(
        i32, (edges, edges), 1
    )
    before = nn(
        jnp.where(mine, 1.0, 0.0).astype(bf16), jnp.where(earlier, 1.0, 0.0).astype(bf16)
    )
    rank = jnp.sum(jnp.where(mine, before, 0.0), axis=0, keepdims=True)
    slot = part * cap + rank.astype(i32)
    slot_ref[...] = slot
    row = lax.broadcasted_iota(i32, (16, edges), 0)
    digits = jnp.where(row == 0, off >> 5, jnp.where(row == 1, off & 31, 0))
    digits = digits.astype(f32).astype(bf16)

    def body(start, width):
        found = nt(digits, ones_at(start, width, slot))
        req_ref[:, pl.ds(start, width)] = (found[0:1] * 32.0 + found[1:2]).astype(i32)

    tiles(owners * cap, body)


def lookup_kernel(cap, ent_ref, off_ref, out_ref, table):
    rows = ent_ref.shape[1]
    table[...] = ent_ref[...].astype(bf16)
    per = TILE // cap

    def step(t, carry):
        start = pl.multiple_of(t * TILE, TILE)
        off = off_ref[:, pl.ds(start, TILE)]
        got = nn(table[...], ones_at(0, rows, off)).astype(bf16)
        for j in range(per):
            out_ref[t * per + j] = got[:, j * cap : (j + 1) * cap]
        return carry

    lax.fori_loop(0, out_ref.shape[0] // per, step, 0)


def query_kernel(ent_ref, rel_ref, src_ref, rid_ref, s_ref, w_ref, q_ref, ent3, rel3):
    dim, rows = ent_ref.shape
    for into, x in ((ent3, ent_ref), (rel3, rel_ref)):
        for k, piece in enumerate(split3(x[...])):
            into[k * dim : (k + 1) * dim] = piece

    def take(table, ids):
        got = nn(table[...], ones_at(0, table.shape[1], ids))
        return got[0:dim] + got[dim : 2 * dim] + got[2 * dim :]

    def body(start, width):
        at = pl.ds(start, width)
        s = take(ent3, src_ref[:, at])
        w = take(rel3, rid_ref[:, at])
        s_ref[:, at] = s
        w_ref[:, at] = w
        q_ref[:, at] = (s * w).astype(bf16)

    tiles(src_ref.shape[1], body)


def score_kernel(cap, q_ref, t_ref, slot_ref, loss_ref, c_ref, tg_ref, tt_ref, logit, top, pos, total):
    slot = slot_ref[...]
    per = TILE // cap
    count = t_ref.shape[0] // per
    top[...] = jnp.full(top.shape, -1e30, f32)
    pos[...] = jnp.zeros(pos.shape, f32)
    total[...] = jnp.zeros(total.shape, f32)

    def first(t, carry):
        start = pl.multiple_of(t * TILE, TILE)
        block = jnp.concatenate([t_ref[t * per + j] for j in range(per)], axis=1)
        tt_ref[:, pl.ds(start, TILE)] = block
        val = tn(block, q_ref[...])
        own = hits(start, TILE, slot)
        used = jnp.max(jnp.where(own, 1.0, 0.0), axis=1, keepdims=True) > 0.5
        val = jnp.where(used, val, -1e30)
        pos[...] += jnp.sum(jnp.where(own, val, 0.0), axis=0, keepdims=True)
        top[...] = jnp.maximum(top[...], jnp.max(val, axis=0, keepdims=True))
        logit[pl.ds(start, TILE)] = val
        return carry

    lax.fori_loop(0, count, first, 0)

    def second(t, carry):
        at = pl.ds(pl.multiple_of(t * TILE, TILE), TILE)
        val = jnp.exp(logit[at] - top[...])
        total[...] += jnp.sum(val, axis=0, keepdims=True)
        logit[at] = val
        return carry

    lax.fori_loop(0, count, second, 0)
    loss_ref[...] = jnp.log(total[...]) + top[...] - pos[...]
    inverse = 1.0 / total[...]

    def third(t, carry):
        start = pl.multiple_of(t * TILE, TILE)
        at = pl.ds(start, TILE)
        prob = logit[at] * inverse
        coef = jnp.where(hits(start, TILE, slot), prob - 1.0, prob).astype(bf16)
        c_ref[at] = coef
        grad = nt(q_ref[...], coef)
        for j in range(per):
            tg_ref[t * per + j] = grad[:, j * cap : (j + 1) * cap].astype(tg_ref.dtype)
        return carry

    lax.fori_loop(0, count, third, 0)


def spread_kernel(tt_ref, c_ref, s_ref, w_ref, src_ref, rid_ref, rel_ref, ent_ref, high2, terms):
    dim = s_ref.shape[0]

    def grads(start, width):
        at = pl.ds(start, width)
        grad = nn(tt_ref[...], c_ref[:, at])
        ent = grad * w_ref[:, at]
        high = ent.astype(bf16)
        high2[0:dim, at] = high
        high2[dim : 2 * dim, at] = (ent - high.astype(f32)).astype(bf16)
        terms[:, at] = (grad * s_ref[:, at]).astype(bf16)

    tiles(s_ref.shape[1], grads)
    pad = rel_ref.shape[0] - dim

    def relation(start, width):
        at = pl.ds(start, width)
        rel_ref[0:dim, at] = nt(terms[...], ones_at(start, width, rid_ref[...])).astype(bf16)
        if pad:
            rel_ref[dim:, at] = jnp.zeros((pad, width), bf16)

    tiles(rel_ref.shape[1], relation)

    def entity(start, width):
        got = nt(high2[...], ones_at(start, width, src_ref[...]))
        ent_ref[:, pl.ds(start, width)] = got[0:dim] + got[dim:]

    tiles(ent_ref.shape[1], entity)


def sum_kernel(owners, chunk, x_ref, out_ref, acc, *rest):
    steps = owners.bit_length() - 1
    boxes = rest[:steps]
    send1, recv1, send2, recv2 = rest[steps:]
    me = lax.axis_index("ent")
    bit = [(me // 2**k) % 2 for k in range(steps)]
    mate = [me + (1 - 2 * bit[k]) * 2**k for k in range(steps)]
    barrier = pltpu.get_barrier_semaphore()
    for k in range(steps):
        pl.semaphore_signal(
            barrier, inc=1, device_id={"ent": mate[k]}, device_id_type=pl.DeviceIdType.MESH
        )
    pl.semaphore_wait(barrier, steps)
    low = 0
    size = owners * chunk
    lows = []
    for k in range(steps):
        lows.append((low, size))
        half = size // 2
        keep = pl.multiple_of(low + bit[k] * half, chunk)
        give = pl.multiple_of(low + (1 - bit[k]) * half, chunk)
        source = x_ref if k == 0 else acc
        copy = pltpu.make_async_remote_copy(
            src_ref=source.at[pl.ds(give, half)],
            dst_ref=boxes[k],
            send_sem=send1.at[k],
            recv_sem=recv1.at[k],
            device_id={"ent": mate[k]},
            device_id_type=pl.DeviceIdType.MESH,
        )
        copy.start()
        copy.wait()
        into = out_ref if k == steps - 1 else acc
        into[pl.ds(keep, half)] = (
            source[pl.ds(keep, half)].astype(f32) + boxes[k][...].astype(f32)
        ).astype(bf16)
        low, size = keep, half
    for k in reversed(range(steps)):
        whole = lows[k][1]
        half = whole // 2
        at = pl.multiple_of(lows[k][0] + bit[k] * half, chunk)
        copy = pltpu.make_async_remote_copy(
            src_ref=out_ref.at[pl.ds(at, half)],
            dst_ref=out_ref.at[pl.ds(at, half)],
            send_sem=send2.at[k],
            recv_sem=recv2.at[k],
            device_id={"ent": mate[k]},
            device_id_type=pl.DeviceIdType.MESH,
        )
        copy.start()
        copy.wait()


def step_rows(value, state, grad):
    after = state + jnp.sum(grad * grad, axis=0, keepdims=True) * (1.0 / grad.shape[0])
    return value - grad * (learn_rate / jnp.sqrt(after)), after


def entity_kernel(cap, arr_ref, off_ref, part_ref, ent_ref, state_ref, new_ref, after_ref, both):
    dim = ent_ref.shape[0]
    per = TILE // cap

    def load(t, carry):
        at = pl.ds(pl.multiple_of(t * TILE, TILE), TILE)
        got = jnp.concatenate([arr_ref[t * per + j] for j in range(per)], axis=1)
        high = got.astype(bf16)
        both[0:dim, at] = high
        both[dim:, at] = (got - high.astype(f32)).astype(bf16)
        return carry

    lax.fori_loop(0, arr_ref.shape[0] // per, load, 0)

    def body(start, width):
        at = pl.ds(start, width)
        got = nt(both[...], ones_at(start, width, off_ref[...]))
        grad = got[0:dim] + got[dim:] + part_ref[:, at]
        new_ref[:, at], after_ref[:, at] = step_rows(ent_ref[:, at], state_ref[:, at], grad)

    tiles(ent_ref.shape[1], body)


def relation_kernel(grad_ref, rel_ref, state_ref, new_ref, after_ref):
    dim = rel_ref.shape[0]

    def body(start, width):
        at = pl.ds(start, width)
        grad = grad_ref[0:dim, at].astype(f32)
        new_ref[:, at], after_ref[:, at] = step_rows(rel_ref[:, at], state_ref[:, at], grad)

    tiles(rel_ref.shape[1], body)


def call(kernel, outs, scratch=(), flops=0, moved=0, **extra):
    shapes = [jax.ShapeDtypeStruct(shape, kind) for shape, kind in outs]
    return pl.pallas_call(
        kernel,
        out_shape=shapes,
        scratch_shapes=list(scratch),
        cost_estimate=pl.CostEstimate(flops=flops, bytes_accessed=moved, transcendentals=0),
        compiler_params=pltpu.CompilerParams(vmem_limit_bytes=48 * 2**20, **extra),
    )


def on_device(
    entity, entity_state, relation, relation_state, src_offset, dst_part, dst_offset, rel_id
):
    rows, dim = entity.shape
    nrel = relation.shape[0]
    edges = src_offset.shape[0]
    assert edges == BLOCK
    owners = lax.axis_size("ent")
    cap = max(2, 2 * edges // owners)
    slots = owners * cap
    chunk = -(-dim // (owners * 16)) * 16
    ent_t, rel_t = entity.T, relation.T
    as_row = lambda x: x.reshape(1, -1)
    src, rid = as_row(src_offset), as_row(rel_id)
    mac = lambda a, b, c: 2 * a * b * c

    slot, requests = call(
        functools.partial(rank_kernel, owners, cap),
        [((1, edges), i32), ((1, slots), i32)],
        flops=mac(16, slots, edges),
        moved=slots * 8,
    )(as_row(dst_part), as_row(dst_offset))
    offsets = lax.all_to_all(
        requests.reshape(owners, cap), "ent", split_axis=0, concat_axis=0, tiled=True
    )
    offsets = as_row(offsets)
    (looked,) = call(
        functools.partial(lookup_kernel, cap),
        [((owners, dim, cap), bf16)],
        [VM((dim, rows), bf16)],
        flops=mac(dim, rows, slots),
        moved=dim * rows * 4,
    )(ent_t, offsets)
    replies = lax.all_to_all(looked, "ent", split_axis=0, concat_axis=0, tiled=True)
    sources, weights, queries = call(
        query_kernel,
        [((dim, edges), f32), ((dim, edges), f32), ((dim, edges), bf16)],
        [VM((3 * dim, rows), bf16), VM((3 * dim, nrel), bf16)],
        flops=mac(3 * dim, rows + nrel, edges),
        moved=dim * nrel * 4,
    )(ent_t, rel_t, src, rid)
    edge_loss, coef, target_grad, targets = call(
        functools.partial(score_kernel, cap),
        [((1, edges), f32), ((slots, edges), bf16), ((owners, dim, cap), f32), ((dim, slots), bf16)],
        [VM((slots, edges), f32)] + [VM((1, edges), f32)] * 3,
        flops=mac(2 * dim, slots, edges),
        moved=slots * edges * 2,
    )(queries, replies, slot)
    arrived = lax.all_to_all(target_grad, "ent", split_axis=0, concat_axis=0, tiled=True)
    relation_terms, entity_part = call(
        spread_kernel,
        [((owners * chunk, nrel), bf16), ((dim, rows), f32)],
        [VM((2 * dim, edges), bf16), VM((dim, edges), bf16)],
        flops=mac(dim, edges, slots + nrel + 2 * rows),
        moved=dim * nrel * 2,
    )(targets, coef, sources, weights, src, rid)
    steps = owners.bit_length() - 1
    (relation_grad,) = call(
        functools.partial(sum_kernel, owners, chunk),
        [((owners * chunk, nrel), bf16)],
        [VM((owners * chunk, nrel), bf16)]
        + [VM(((owners * chunk) >> (k + 1), nrel), bf16) for k in range(steps)]
        + [pltpu.SemaphoreType.DMA((steps,))] * 4,
        moved=dim * nrel * 8,
        collective_id=0,
        has_side_effects=True,
    )(relation_terms)
    new_rel, rel_after = call(
        relation_kernel, [((dim, nrel), f32), ((1, nrel), f32)], moved=dim * nrel * 10
    )(relation_grad, rel_t, as_row(relation_state))
    new_ent, ent_after = call(
        functools.partial(entity_kernel, cap),
        [((dim, rows), f32), ((1, rows), f32)],
        [VM((2 * dim, slots), bf16)],
        flops=mac(2 * dim, slots, rows),
        moved=dim * rows * 8,
    )(arrived, offsets, entity_part, ent_t, as_row(entity_state))
    return (
        new_ent.T,
        ent_after.reshape(rows),
        new_rel.T,
        rel_after.reshape(nrel),
        edge_loss.reshape(edges),
    )


def solution(mesh):
    placed = (
        P(("groups", "ent"), None),
        P(("groups", "ent")),
        P("groups", None),
        P("groups"),
        P(("groups", "ent")),
        P(("groups", "ent"), None),
        P(("groups", "ent")),
        P(("groups", "ent")),
    )
    return jax.shard_map(
        on_device,
        mesh=mesh,
        in_specs=placed,
        out_specs=(
            P(("groups", "ent"), None),
            P(("groups", "ent")),
            P("groups", None),
            P("groups"),
            P(("groups", "ent")),
        ),
        check_vma=False,
    )
```

```python
import functools

import jax
import jax.numpy as jnp
from jax import lax
from jax.experimental import pallas as pl
from jax.experimental.pallas import tpu as pltpu
from jax.sharding import PartitionSpec as P

BLOCK = 1024
TILE = 256
learn_rate = 0.3

f32, bf16, i32 = jnp.float32, jnp.bfloat16, jnp.int32
VM = pltpu.VMEM


def nt(a, b):
    return lax.dot_general(a, b, (((1,), (1,)), ((), ())), preferred_element_type=f32)


def tn(a, b):
    return lax.dot_general(a, b, (((0,), (0,)), ((), ())), preferred_element_type=f32)


def nn(a, b):
    return jnp.dot(a, b, preferred_element_type=f32)


def hits(first, count, row):
    return lax.broadcasted_iota(i32, (count, row.shape[1]), 0) + first == row


def ones_at(first, count, row):
    return jnp.where(hits(first, count, row), 1.0, 0.0).astype(bf16)


def tiles(total, body, size=TILE):
    whole = total // size

    def step(t, carry):
        body(pl.multiple_of(t * size, size), size)
        return carry

    lax.fori_loop(0, whole, step, 0)
    if total % size:
        body(whole * size, total % size)


def split3(x):
    high = x.astype(bf16)
    rest = x - high.astype(f32)
    mid = rest.astype(bf16)
    return high, mid, (rest - mid.astype(f32)).astype(bf16)


MESH = pl.DeviceIdType.MESH


def greet(owners, me):
    barrier = pltpu.get_barrier_semaphore()

    def step(d, carry):
        pl.semaphore_signal(
            barrier, inc=1, device_id={"ent": (me + d) % owners}, device_id_type=MESH
        )
        return carry

    lax.fori_loop(1, owners, step, 0)
    return barrier


def swap(owners, me, source, target, send, recv):
    def copy(d):
        other = (me + d) % owners
        return pltpu.make_async_remote_copy(
            src_ref=source.at[other],
            dst_ref=target.at[me],
            send_sem=send.at[d],
            recv_sem=recv.at[d],
            device_id={"ent": other},
            device_id_type=MESH,
        )

    return copy


def each_peer(owners, body):
    def step(t, carry):
        body(1 + (owners // 2 - 1 + t) % (owners - 1))
        return carry

    lax.fori_loop(0, owners - 1, step, 0)


def fetch_kernel(
    owners, cap, part_ref, off_ref, ent_ref, rel_ref, src_ref, rid_ref,
    slot_ref, asked_ref, t_ref, s_ref, w_ref, q_ref,
    request, found, ent3, rel3, send1, recv1, send2, recv2,
):
    me = lax.axis_index("ent")
    barrier = greet(owners, me)
    dim, rows = ent_ref.shape
    part, off = part_ref[...], off_ref[...]
    edges = part.shape[1]
    mine = hits(0, owners, part)
    earlier = lax.broadcasted_iota(i32, (edges, edges), 0) < lax.broadcasted_iota(
        i32, (edges, edges), 1
    )
    before = nn(
        jnp.where(mine, 1.0, 0.0).astype(bf16), jnp.where(earlier, 1.0, 0.0).astype(bf16)
    )
    rank = jnp.sum(jnp.where(mine, before, 0.0), axis=0, keepdims=True)
    slot = part * cap + rank.astype(i32)
    slot_ref[...] = slot
    row = lax.broadcasted_iota(i32, (16, edges), 0)
    digits = jnp.where(row == 0, off >> 5, jnp.where(row == 1, off & 31, 0))
    digits = digits.astype(f32).astype(bf16)
    per = TILE // cap

    def ask(t, carry):
        got = nt(digits, ones_at(t * TILE, TILE, slot))
        got = (got[0:1] * 32.0 + got[1:2]).astype(i32)
        for j in range(per):
            request[t * per + j] = jnp.broadcast_to(got[:, j * cap : (j + 1) * cap], (8, cap))
        return carry

    lax.fori_loop(0, owners // per, ask, 0)
    pl.semaphore_wait(barrier, owners - 1)
    ids = swap(owners, me, request, asked_ref, send1, recv1)
    each_peer(owners, lambda d: ids(d).start())
    asked_ref[me] = request[me]
    for k, piece in enumerate(split3(ent_ref[...])):
        ent3[k * dim : (k + 1) * dim] = piece

    def look(owner):
        found[owner] = nn(ent3[0:dim], ones_at(0, rows, asked_ref[owner][0:1])).astype(bf16)

    each_peer(owners, lambda d: ids(d).wait())
    rows_out = swap(owners, me, found, t_ref, send2, recv2)

    def reply(d):
        look((me + d) % owners)
        rows_out(d).start()

    each_peer(owners, reply)
    look(me)
    t_ref[me] = found[me]

    for k, piece in enumerate(split3(rel_ref[...])):
        rel3[k * dim : (k + 1) * dim] = piece

    def take(table, ids_row):
        got = nn(table[...], ones_at(0, table.shape[1], ids_row))
        return got[0:dim] + got[dim : 2 * dim] + got[2 * dim :]

    def body(start, width):
        at = pl.ds(start, width)
        s = take(ent3, src_ref[:, at])
        w = take(rel3, rid_ref[:, at])
        s_ref[:, at] = s
        w_ref[:, at] = w
        q_ref[:, at] = (s * w).astype(bf16)

    tiles(edges, body)
    each_peer(owners, lambda d: rows_out(d).wait())


def quantum(power):
    return jnp.exp2(power) * (1.0 / 32000.0)


def encode(x):
    power = jnp.ceil(jnp.log2(jnp.maximum(jnp.max(jnp.abs(x), axis=0, keepdims=True), 1e-30)))
    return jnp.floor(x * (1.0 / quantum(power)) + 0.5), power


def short(x):
    return x.astype(i32).astype(jnp.int16)


def wide(x):
    return x.astype(i32).astype(f32)


def score_kernel(cap, q_ref, t_ref, slot_ref, loss_ref, c_ref, tg_ref, tt_ref, logit, top, pos, total):
    slot = slot_ref[...]
    per = TILE // cap
    count = t_ref.shape[0] // per
    top[...] = jnp.full(top.shape, -1e30, f32)
    pos[...] = jnp.zeros(pos.shape, f32)
    total[...] = jnp.zeros(total.shape, f32)

    def first(t, carry):
        start = pl.multiple_of(t * TILE, TILE)
        block = jnp.concatenate([t_ref[t * per + j] for j in range(per)], axis=1)
        tt_ref[:, pl.ds(start, TILE)] = block
        val = tn(block, q_ref[...])
        own = hits(start, TILE, slot)
        used = jnp.max(jnp.where(own, 1.0, 0.0), axis=1, keepdims=True) > 0.5
        val = jnp.where(used, val, -1e30)
        pos[...] += jnp.sum(jnp.where(own, val, 0.0), axis=0, keepdims=True)
        top[...] = jnp.maximum(top[...], jnp.max(val, axis=0, keepdims=True))
        logit[pl.ds(start, TILE)] = val
        return carry

    lax.fori_loop(0, count, first, 0)

    def second(t, carry):
        at = pl.ds(pl.multiple_of(t * TILE, TILE), TILE)
        val = jnp.exp(logit[at] - top[...])
        total[...] += jnp.sum(val, axis=0, keepdims=True)
        logit[at] = val
        return carry

    lax.fori_loop(0, count, second, 0)
    loss_ref[...] = jnp.log(total[...]) + top[...] - pos[...]
    inverse = 1.0 / total[...]

    def third(t, carry):
        start = pl.multiple_of(t * TILE, TILE)
        at = pl.ds(start, TILE)
        prob = logit[at] * inverse
        coef = jnp.where(hits(start, TILE, slot), prob - 1.0, prob).astype(bf16)
        c_ref[at] = coef
        grad, power = encode(nt(q_ref[...], coef))
        code = short(jnp.concatenate([grad, jnp.broadcast_to(power, (16, TILE))], axis=0))
        for j in range(per):
            tg_ref[t * per + j] = code[:, j * cap : (j + 1) * cap]
        return carry

    lax.fori_loop(0, count, third, 0)


def return_kernel(
    owners, cap, share, tg_ref, tt_ref, c_ref, s_ref, w_ref, src_ref, rid_ref, asked_ref,
    ent_ref, state_ref, new_ref, after_ref, out_ref,
    arrived, high2, terms2, acc, part, both, *rest,
):
    steps = owners.bit_length() - 1
    boxes, bags = rest[:steps], rest[steps : 2 * steps]
    send0, recv0, send1, recv1, send2, recv2 = rest[2 * steps :]
    me = lax.axis_index("ent")
    barrier = greet(owners, me)
    pl.semaphore_wait(barrier, owners - 1)
    grads_out = swap(owners, me, tg_ref, arrived, send0, recv0)
    each_peer(owners, lambda d: grads_out(d).start())
    arrived[me] = tg_ref[me]

    dim, edges = s_ref.shape
    chunk = acc.shape[1]

    def halves(into, at, x):
        high = x.astype(bf16)
        into[0:dim, at] = high
        into[dim : 2 * dim, at] = (x - high.astype(f32)).astype(bf16)

    def grads(start, width):
        at = pl.ds(start, width)
        grad = nn(tt_ref[...], c_ref[:, at])
        halves(high2, at, grad * w_ref[:, at])
        halves(terms2, at, grad * s_ref[:, at])

    tiles(edges, grads)

    def relation(start, width):
        at = pl.ds(start, width)
        got = nt(terms2[...], ones_at(start, width, rid_ref[...]))
        got = got[0:dim] + got[dim:]
        for c in range(owners):
            low, high = min(c * share, dim), min((c + 1) * share, dim)
            gap = jnp.zeros((chunk - (high - low), width), f32)
            acc[c, :, at] = jnp.concatenate([got[low:high], gap], axis=0) if high > low else gap

    tiles(acc.shape[2], relation)

    def pack(c):
        code, power = encode(acc[c])
        last = lax.broadcasted_iota(i32, code.shape, 0) == chunk - 1
        return short(jnp.where(last, power, code))

    def entity_part(start, width):
        got = nt(high2[...], ones_at(start, width, src_ref[...]))
        part[:, pl.ds(start, width)] = got[0:dim] + got[dim:]

    def entity_all():
        each_peer(owners, lambda d: grads_out(d).wait())
        per = TILE // cap

        def load(t, carry):
            got = jnp.concatenate([arrived[t * per + j] for j in range(per)], axis=1)
            got = wide(got)
            got = got[0:dim] * quantum(got[dim : dim + 1])
            halves(both, pl.ds(pl.multiple_of(t * TILE, TILE), TILE), got)
            return carry

        lax.fori_loop(0, owners // per, load, 0)
        asked = jnp.concatenate([asked_ref[p][0:1] for p in range(owners)], axis=1)

        def body(start, width):
            at = pl.ds(start, width)
            got = nt(both[...], ones_at(start, width, asked))
            grad = got[0:dim] + got[dim:] + part[:, at]
            new_ref[:, at], after_ref[:, at] = step_rows(ent_ref[:, at], state_ref[:, at], grad)

        tiles(ent_ref.shape[1], body)

    def remote(source, target, mate, send, recv):
        return pltpu.make_async_remote_copy(
            src_ref=source, dst_ref=target, send_sem=send, recv_sem=recv,
            device_id={"ent": mate}, device_id_type=MESH,
        )

    bit = [(me // 2**k) % 2 for k in range(steps)]
    mate = [me + (1 - 2 * bit[k]) * 2**k for k in range(steps)]
    low, size, lows = 0, owners, []
    for k in range(steps):
        lows.append((low, size))
        half = size // 2
        keep, give = low + bit[k] * half, low + (1 - bit[k]) * half

        def fill(c, carry):
            bags[k][c] = pack(give + c)
            return carry

        lax.fori_loop(0, half, fill, 0)
        copy = remote(bags[k], boxes[k], mate[k], send1.at[k], recv1.at[k])
        copy.start()
        if k == 0:
            tiles(ent_ref.shape[1], entity_part)
        copy.wait()

        def add(c, carry):
            got = wide(boxes[k][c])
            body = got * quantum(got[chunk - 1 :])
            last = lax.broadcasted_iota(i32, got.shape, 0) == chunk - 1
            acc[keep + c] = acc[keep + c] + jnp.where(last, 0.0, body)
            return carry

        lax.fori_loop(0, half, add, 0)
        low, size = keep, half
    out_ref[low] = pack(low)
    for k in reversed(range(steps)):
        half = lows[k][1] // 2
        place = out_ref.at[pl.ds(lows[k][0] + bit[k] * half, half)]
        copy = remote(place, place, mate[k], send2.at[k], recv2.at[k])
        copy.start()
        if k == min(1, steps - 1):
            entity_all()
        copy.wait()


def step_rows(value, state, grad):
    after = state + jnp.sum(grad * grad, axis=0, keepdims=True) * (1.0 / grad.shape[0])
    return value - grad * (learn_rate / jnp.sqrt(after)), after


def relation_kernel(share, code_ref, rel_ref, state_ref, new_ref, after_ref):
    dim = rel_ref.shape[0]

    def body(start, width):
        at = pl.ds(start, width)
        pieces = []
        for c in range(-(-dim // share)):
            got = wide(code_ref[c, :, at])
            used = min(share, dim - c * share)
            pieces.append(got[0:used] * quantum(got[code_ref.shape[1] - 1 :]))
        grad = jnp.concatenate(pieces, axis=0)
        new_ref[:, at], after_ref[:, at] = step_rows(rel_ref[:, at], state_ref[:, at], grad)

    tiles(rel_ref.shape[1], body)


def call(kernel, outs, scratch=(), flops=0, moved=0, **extra):
    shapes = [jax.ShapeDtypeStruct(shape, kind) for shape, kind in outs]
    return pl.pallas_call(
        kernel,
        out_shape=shapes,
        scratch_shapes=list(scratch),
        cost_estimate=pl.CostEstimate(flops=flops, bytes_accessed=moved, transcendentals=0),
        compiler_params=pltpu.CompilerParams(vmem_limit_bytes=56 * 2**20, **extra),
    )


def on_device(
    entity, entity_state, relation, relation_state, src_offset, dst_part, dst_offset, rel_id
):
    rows, dim = entity.shape
    nrel = relation.shape[0]
    edges = src_offset.shape[0]
    assert edges == BLOCK
    owners = lax.axis_size("ent")
    cap = max(2, 2 * edges // owners)
    slots = owners * cap
    share = -(-dim // owners)
    chunk = -(-(share + 1) // 16) * 16
    steps = owners.bit_length() - 1
    assert owners == 2**steps
    ent_t, rel_t = entity.T, relation.T
    as_row = lambda x: x.reshape(1, -1)
    src, rid = as_row(src_offset), as_row(rel_id)
    mac = lambda a, b, c: 2 * a * b * c
    dma = pltpu.SemaphoreType.DMA

    slot, asked, replies, sources, weights, queries = call(
        functools.partial(fetch_kernel, owners, cap),
        [
            ((1, edges), i32), ((owners, 8, cap), i32), ((owners, dim, cap), bf16),
            ((dim, edges), f32), ((dim, edges), f32), ((dim, edges), bf16),
        ],
        [
            VM((owners, 8, cap), i32), VM((owners, dim, cap), bf16),
            VM((3 * dim, rows), bf16), VM((3 * dim, nrel), bf16),
        ]
        + [dma((owners,))] * 4,
        flops=mac(3 * dim, rows + nrel, edges) + mac(dim, rows, slots),
        moved=dim * nrel * 8,
        collective_id=0,
        has_side_effects=True,
    )(as_row(dst_part), as_row(dst_offset), ent_t, rel_t, src, rid)
    edge_loss, coef, target_grad, targets = call(
        functools.partial(score_kernel, cap),
        [
            ((1, edges), f32), ((slots, edges), bf16),
            ((owners, dim + 16, cap), jnp.int16), ((dim, slots), bf16),
        ],
        [VM((slots, edges), f32)] + [VM((1, edges), f32)] * 3,
        flops=mac(2 * dim, slots, edges),
        moved=slots * edges * 2,
    )(queries, replies, slot)
    half = [VM((owners >> (k + 1), chunk, nrel), jnp.int16) for k in range(steps)]
    new_ent, ent_after, relation_code = call(
        functools.partial(return_kernel, owners, cap, share),
        [((dim, rows), f32), ((1, rows), f32), ((owners, chunk, nrel), jnp.int16)],
        [
            VM((owners, dim + 16, cap), jnp.int16), VM((2 * dim, edges), bf16),
            VM((2 * dim, edges), bf16), VM((owners, chunk, nrel), f32),
            VM((dim, rows), f32), VM((2 * dim, slots), bf16),
        ]
        + half + half + [dma((owners,))] * 2 + [dma((steps,))] * 4,
        flops=mac(dim, edges, slots + 2 * nrel + 2 * rows) + mac(2 * dim, slots, rows),
        moved=dim * nrel * 8,
        collective_id=1,
        has_side_effects=True,
    )(target_grad, targets, coef, sources, weights, src, rid, asked, ent_t, as_row(entity_state))
    new_rel, rel_after = call(
        functools.partial(relation_kernel, share),
        [((dim, nrel), f32), ((1, nrel), f32)],
        moved=dim * nrel * 10,
    )(relation_code, rel_t, as_row(relation_state))
    return (
        new_ent.T,
        ent_after.reshape(rows),
        new_rel.T,
        rel_after.reshape(nrel),
        edge_loss.reshape(edges),
    )


def solution(mesh):
    placed = (
        P(("groups", "ent"), None),
        P(("groups", "ent")),
        P("groups", None),
        P("groups"),
        P(("groups", "ent")),
        P(("groups", "ent"), None),
        P(("groups", "ent")),
        P(("groups", "ent")),
    )
    return jax.shard_map(
        on_device,
        mesh=mesh,
        in_specs=placed,
        out_specs=(
            P(("groups", "ent"), None),
            P(("groups", "ent")),
            P("groups", None),
            P("groups"),
            P(("groups", "ent")),
        ),
        check_vma=False,
    )
```

```python
import functools

import jax
import jax.numpy as jnp
from jax import lax
from jax.experimental import pallas as pl
from jax.experimental.pallas import tpu as pltpu
from jax.sharding import PartitionSpec as P

BLOCK = 1024
TILE = 256
learn_rate = 0.3

f32, bf16, i32 = jnp.float32, jnp.bfloat16, jnp.int32
VM = pltpu.VMEM


def nt(a, b):
    return lax.dot_general(a, b, (((1,), (1,)), ((), ())), preferred_element_type=f32)


def tn(a, b):
    return lax.dot_general(a, b, (((0,), (0,)), ((), ())), preferred_element_type=f32)


def nn(a, b):
    return jnp.dot(a, b, preferred_element_type=f32)


def hits(first, count, row):
    return lax.broadcasted_iota(i32, (count, row.shape[1]), 0) + first == row


def ones_at(first, count, row):
    return jnp.where(hits(first, count, row), 1.0, 0.0).astype(bf16)


def tiles(total, body, size=TILE):
    whole = total // size

    def step(t, carry):
        body(pl.multiple_of(t * size, size), size)
        return carry

    lax.fori_loop(0, whole, step, 0)
    if total % size:
        body(whole * size, total % size)


def split3(x):
    high = x.astype(bf16)
    rest = x - high.astype(f32)
    mid = rest.astype(bf16)
    return high, mid, (rest - mid.astype(f32)).astype(bf16)


MESH = pl.DeviceIdType.MESH


def greet(owners, me):
    barrier = pltpu.get_barrier_semaphore()

    def step(d, carry):
        pl.semaphore_signal(
            barrier, inc=1, device_id={"ent": (me + d) % owners}, device_id_type=MESH
        )
        return carry

    lax.fori_loop(1, owners, step, 0)
    return barrier


def swap(owners, me, source, target, send, recv):
    def copy(d):
        other = (me + d) % owners
        return pltpu.make_async_remote_copy(
            src_ref=source.at[other],
            dst_ref=target.at[me],
            send_sem=send.at[d],
            recv_sem=recv.at[d],
            device_id={"ent": other},
            device_id_type=MESH,
        )

    return copy


def each_peer(owners, body, first=1):
    def step(t, carry):
        body(1 + (first - 1 + t) % (owners - 1))
        return carry

    lax.fori_loop(0, owners - 1, step, 0)


def fetch_kernel(
    owners, cap, part_ref, off_ref, ent_ref, rel_ref, src_ref, rid_ref,
    slot_ref, asked_ref, t_ref, s_ref, w_ref, q_ref,
    request, found, ent3, rel3, send1, recv1, send2, recv2,
):
    me = lax.axis_index("ent")
    barrier = greet(owners, me)
    dim, rows = ent_ref.shape
    part, off = part_ref[...], off_ref[...]
    edges = part.shape[1]
    mine = hits(0, owners, part)
    earlier = lax.broadcasted_iota(i32, (edges, edges), 0) < lax.broadcasted_iota(
        i32, (edges, edges), 1
    )
    before = nn(
        jnp.where(mine, 1.0, 0.0).astype(bf16), jnp.where(earlier, 1.0, 0.0).astype(bf16)
    )
    rank = jnp.sum(jnp.where(mine, before, 0.0), axis=0, keepdims=True)
    slot = part * cap + rank.astype(i32)
    slot_ref[...] = slot
    row = lax.broadcasted_iota(i32, (16, edges), 0)
    digits = jnp.where(row == 0, off >> 5, jnp.where(row == 1, off & 31, 0))
    digits = digits.astype(f32).astype(bf16)
    per = TILE // cap

    def ask(t, carry):
        got = nt(digits, ones_at(t * TILE, TILE, slot))
        got = (got[0:1] * 32.0 + got[1:2]).astype(i32)
        for j in range(per):
            request[t * per + j] = jnp.broadcast_to(got[:, j * cap : (j + 1) * cap], (8, cap))
        return carry

    lax.fori_loop(0, owners // per, ask, 0)
    pl.semaphore_wait(barrier, owners - 1)
    ids = swap(owners, me, request, asked_ref, send1, recv1)
    each_peer(owners, lambda d: ids(d).start())
    asked_ref[me] = request[me]
    for k, piece in enumerate(split3(ent_ref[...])):
        ent3[k * dim : (k + 1) * dim] = piece

    def look(owner):
        found[owner] = nn(ent3[0:dim], ones_at(0, rows, asked_ref[owner][0:1])).astype(bf16)

    each_peer(owners, lambda d: ids(d).wait())
    rows_out = swap(owners, me, found, t_ref, send2, recv2)

    def reply(d):
        look((me + d) % owners)
        rows_out(d).start()

    each_peer(owners, reply)
    look(me)
    t_ref[me] = found[me]

    for k, piece in enumerate(split3(rel_ref[...])):
        rel3[k * dim : (k + 1) * dim] = piece

    def take(table, ids_row):
        got = nn(table[...], ones_at(0, table.shape[1], ids_row))
        return got[0:dim] + got[dim : 2 * dim] + got[2 * dim :]

    def body(start, width):
        at = pl.ds(start, width)
        s = take(ent3, src_ref[:, at])
        w = take(rel3, rid_ref[:, at])
        s_ref[:, at] = s
        w_ref[:, at] = w
        q_ref[:, at] = (s * w).astype(bf16)

    tiles(edges, body)
    each_peer(owners, lambda d: rows_out(d).wait())


def quantum(power):
    return jnp.exp2(power) * (1.0 / 32000.0)


def encode(x):
    power = jnp.ceil(jnp.log2(jnp.maximum(jnp.max(jnp.abs(x), axis=0, keepdims=True), 1e-30)))
    return jnp.floor(x * (1.0 / quantum(power)) + 0.5), power


def short(x):
    return x.astype(i32).astype(jnp.int16)


def wide(x):
    return x.astype(i32).astype(f32)


def score_kernel(cap, q_ref, t_ref, slot_ref, loss_ref, c_ref, tg_ref, tt_ref, logit, top, pos, total):
    slot = slot_ref[...]
    per = TILE // cap
    count = t_ref.shape[0] // per
    top[...] = jnp.full(top.shape, -1e30, f32)
    pos[...] = jnp.zeros(pos.shape, f32)
    total[...] = jnp.zeros(total.shape, f32)

    def first(t, carry):
        start = pl.multiple_of(t * TILE, TILE)
        block = jnp.concatenate([t_ref[t * per + j] for j in range(per)], axis=1)
        tt_ref[:, pl.ds(start, TILE)] = block
        val = tn(block, q_ref[...])
        own = hits(start, TILE, slot)
        used = jnp.max(jnp.where(own, 1.0, 0.0), axis=1, keepdims=True) > 0.5
        val = jnp.where(used, val, -1e30)
        pos[...] += jnp.sum(jnp.where(own, val, 0.0), axis=0, keepdims=True)
        top[...] = jnp.maximum(top[...], jnp.max(val, axis=0, keepdims=True))
        logit[pl.ds(start, TILE)] = val
        return carry

    lax.fori_loop(0, count, first, 0)

    def second(t, carry):
        at = pl.ds(pl.multiple_of(t * TILE, TILE), TILE)
        val = jnp.exp(logit[at] - top[...])
        total[...] += jnp.sum(val, axis=0, keepdims=True)
        logit[at] = val
        return carry

    lax.fori_loop(0, count, second, 0)
    loss_ref[...] = jnp.log(total[...]) + top[...] - pos[...]
    inverse = 1.0 / total[...]

    def third(t, carry):
        start = pl.multiple_of(t * TILE, TILE)
        at = pl.ds(start, TILE)
        prob = logit[at] * inverse
        coef = jnp.where(hits(start, TILE, slot), prob - 1.0, prob).astype(bf16)
        c_ref[at] = coef
        grad, power = encode(nt(q_ref[...], coef))
        code = short(jnp.concatenate([grad, jnp.broadcast_to(power, (16, TILE))], axis=0))
        for j in range(per):
            tg_ref[t * per + j] = code[:, j * cap : (j + 1) * cap]
        return carry

    lax.fori_loop(0, count, third, 0)


def return_kernel(
    owners, cap, share, pieces, tg_ref, tt_ref, c_ref, s_ref, w_ref, src_ref, rid_ref, asked_ref,
    ent_ref, state_ref, new_ref, after_ref, *rest,
):
    steps = owners.bit_length() - 1
    count = len(pieces)
    outs, rest = rest[:count], rest[count:]
    arrived, high2, terms2, part, both, send0, recv0, send1, recv1, send2, recv2 = rest[:11]
    accs, rest = rest[11 : 11 + count], rest[11 + count :]
    boxes = [rest[p * steps : (p + 1) * steps] for p in range(count)]
    rest = rest[count * steps :]
    bags = [rest[p * steps : (p + 1) * steps] for p in range(count)]
    me = lax.axis_index("ent")
    barrier = greet(owners, me)
    pl.semaphore_wait(barrier, owners - 1)
    grads_out = swap(owners, me, tg_ref, arrived, send0, recv0)
    each_peer(owners, lambda d: grads_out(d).start(), owners // 2)
    arrived[me] = tg_ref[me]

    dim, edges = s_ref.shape
    chunk = accs[0].shape[1]

    def halves(into, at, x):
        high = x.astype(bf16)
        into[0:dim, at] = high
        into[dim : 2 * dim, at] = (x - high.astype(f32)).astype(bf16)

    def grads(start, width):
        at = pl.ds(start, width)
        grad = nn(tt_ref[...], c_ref[:, at])
        halves(high2, at, grad * w_ref[:, at])
        halves(terms2, at, grad * s_ref[:, at])

    tiles(edges, grads)

    def relation(p, start, width):
        acc = accs[p]
        at = pl.ds(start, width)
        got = nt(terms2[...], ones_at(pieces[p][0] + start, width, rid_ref[...]))
        got = got[0:dim] + got[dim:]
        for c in range(owners):
            low, high = min(c * share, dim), min((c + 1) * share, dim)
            gap = jnp.zeros((chunk - (high - low), width), f32)
            acc[c, :, at] = jnp.concatenate([got[low:high], gap], axis=0) if high > low else gap

    def pack(p, c):
        code, power = encode(accs[p][c])
        last = lax.broadcasted_iota(i32, code.shape, 0) == chunk - 1
        return short(jnp.where(last, power, code))

    def entity_part(start, width):
        got = nt(high2[...], ones_at(start, width, src_ref[...]))
        part[:, pl.ds(start, width)] = got[0:dim] + got[dim:]

    def entity_all():
        each_peer(owners, lambda d: grads_out(d).wait())
        per = TILE // cap

        def load(t, carry):
            got = jnp.concatenate([arrived[t * per + j] for j in range(per)], axis=1)
            got = wide(got)
            got = got[0:dim] * quantum(got[dim : dim + 1])
            halves(both, pl.ds(pl.multiple_of(t * TILE, TILE), TILE), got)
            return carry

        lax.fori_loop(0, owners // per, load, 0)
        asked = jnp.concatenate([asked_ref[p][0:1] for p in range(owners)], axis=1)

        def body(start, width):
            at = pl.ds(start, width)
            got = nt(both[...], ones_at(start, width, asked))
            grad = got[0:dim] + got[dim:] + part[:, at]
            new_ref[:, at], after_ref[:, at] = step_rows(ent_ref[:, at], state_ref[:, at], grad)

        tiles(ent_ref.shape[1], body)

    def remote(source, target, mate, send, recv):
        return pltpu.make_async_remote_copy(
            src_ref=source, dst_ref=target, send_sem=send, recv_sem=recv,
            device_id={"ent": mate}, device_id_type=MESH,
        )

    bit = [(me // 2**k) % 2 for k in range(steps)]
    mate = [me + (1 - 2 * bit[k]) * 2**k for k in range(steps)]
    place = [(0, owners)] * count
    past = [[] for _ in pieces]
    flying = [None] * count

    def give(p, k):
        b = pieces[p][2][k]
        low, size = place[p]
        half = size // 2
        past[p].append((low, size))
        away = low + (1 - bit[b]) * half

        def fill(c, carry):
            bags[p][k][c] = pack(p, away + c)
            return carry

        lax.fori_loop(0, half, fill, 0)
        at = p * steps + k
        flying[p] = remote(bags[p][k], boxes[p][k], mate[b], send1.at[at], recv1.at[at])
        flying[p].start()
        place[p] = (low + bit[b] * half, half)

    def take(p, k):
        flying[p].wait()
        low, half = place[p]

        def add(c, carry):
            got = wide(boxes[p][k][c])
            body = got * quantum(got[chunk - 1 :])
            last = lax.broadcasted_iota(i32, got.shape, 0) == chunk - 1
            accs[p][low + c] = accs[p][low + c] + jnp.where(last, 0.0, body)
            return carry

        lax.fori_loop(0, half, add, 0)

    def share_out(p, k):
        b = pieces[p][2][k]
        low, size = past[p][k]
        here = outs[p].at[pl.ds(low + bit[b] * (size // 2), size // 2)]
        at = p * steps + k
        flying[p] = remote(here, here, mate[b], send2.at[at], recv2.at[at])
        flying[p].start()

    for p in range(count):
        tiles(pieces[p][1], functools.partial(relation, p))
        give(p, 0)
    tiles(ent_ref.shape[1], entity_part)
    for k in range(steps):
        for p in range(count):
            take(p, k)
            if k < steps - 1:
                give(p, k + 1)
            else:
                outs[p][place[p][0]] = pack(p, place[p][0])
                share_out(p, k)
    for k in reversed(range(steps)):
        if k == min(1, steps - 1):
            entity_all()
        for p in range(count):
            flying[p].wait()
            if k:
                share_out(p, k - 1)


def step_rows(value, state, grad):
    after = state + jnp.sum(grad * grad, axis=0, keepdims=True) * (1.0 / grad.shape[0])
    return value - grad * (learn_rate / jnp.sqrt(after)), after


def relation_kernel(share, pieces, *refs):
    codes, (rel_ref, state_ref, new_ref, after_ref) = refs[:-4], refs[-4:]
    dim = rel_ref.shape[0]
    chunk = codes[0].shape[1]

    def body(p, start, width):
        found = []
        for c in range(-(-dim // share)):
            got = wide(codes[p][c, :, pl.ds(start, width)])
            used = min(share, dim - c * share)
            found.append(got[0:used] * quantum(got[chunk - 1 :]))
        grad = jnp.concatenate(found, axis=0)
        at = pl.ds(pieces[p][0] + start, width)
        new_ref[:, at], after_ref[:, at] = step_rows(rel_ref[:, at], state_ref[:, at], grad)

    for p in range(len(pieces)):
        tiles(pieces[p][1], functools.partial(body, p))


def call(kernel, outs, scratch=(), flops=0, moved=0, **extra):
    shapes = [jax.ShapeDtypeStruct(shape, kind) for shape, kind in outs]
    return pl.pallas_call(
        kernel,
        out_shape=shapes,
        scratch_shapes=list(scratch),
        cost_estimate=pl.CostEstimate(flops=flops, bytes_accessed=moved, transcendentals=0),
        compiler_params=pltpu.CompilerParams(vmem_limit_bytes=56 * 2**20, **extra),
    )


def on_device(
    entity, entity_state, relation, relation_state, src_offset, dst_part, dst_offset, rel_id
):
    rows, dim = entity.shape
    nrel = relation.shape[0]
    edges = src_offset.shape[0]
    assert edges == BLOCK
    owners = lax.axis_size("ent")
    cap = max(2, 2 * edges // owners)
    slots = owners * cap
    share = -(-dim // owners)
    chunk = -(-(share + 1) // 16) * 16
    steps = owners.bit_length() - 1
    assert owners == 2**steps
    ent_t, rel_t = entity.T, relation.T
    as_row = lambda x: x.reshape(1, -1)
    src, rid = as_row(src_offset), as_row(rel_id)
    mac = lambda a, b, c: 2 * a * b * c
    dma = pltpu.SemaphoreType.DMA

    slot, asked, replies, sources, weights, queries = call(
        functools.partial(fetch_kernel, owners, cap),
        [
            ((1, edges), i32), ((owners, 8, cap), i32), ((owners, dim, cap), bf16),
            ((dim, edges), f32), ((dim, edges), f32), ((dim, edges), bf16),
        ],
        [
            VM((owners, 8, cap), i32), VM((owners, dim, cap), bf16),
            VM((3 * dim, rows), bf16), VM((3 * dim, nrel), bf16),
        ]
        + [dma((owners,))] * 4,
        flops=mac(3 * dim, rows + nrel, edges) + mac(dim, rows, slots),
        moved=dim * nrel * 8,
        collective_id=0,
        has_side_effects=True,
    )(as_row(dst_part), as_row(dst_offset), ent_t, rel_t, src, rid)
    edge_loss, coef, target_grad, targets = call(
        functools.partial(score_kernel, cap),
        [
            ((1, edges), f32), ((slots, edges), bf16),
            ((owners, dim + 16, cap), jnp.int16), ((dim, slots), bf16),
        ],
        [VM((slots, edges), f32)] + [VM((1, edges), f32)] * 3,
        flops=mac(2 * dim, slots, edges),
        moved=slots * edges * 2,
    )(queries, replies, slot)
    first = -(-nrel // 256) * 128
    order = list(range(steps))
    other = order[:1] + order[2:] + order[1:2]
    pieces = [(0, first, order), (first, nrel - first, other)]
    half = [
        VM((owners >> (k + 1), chunk, wide_), jnp.int16) for _, wide_, _ in pieces for k in range(steps)
    ]
    new_ent, ent_after, *codes = call(
        functools.partial(return_kernel, owners, cap, share, pieces),
        [((dim, rows), f32), ((1, rows), f32)]
        + [((owners, chunk, wide_), jnp.int16) for _, wide_, _ in pieces],
        [
            VM((owners, dim + 16, cap), jnp.int16), VM((2 * dim, edges), bf16),
            VM((2 * dim, edges), bf16), VM((dim, rows), f32), VM((2 * dim, slots), bf16),
        ]
        + [dma((owners,))] * 2
        + [dma((len(pieces) * steps,))] * 4
        + [VM((owners, chunk, wide_), f32) for _, wide_, _ in pieces]
        + half
        + half,
        flops=mac(dim, edges, slots + 2 * nrel + 2 * rows) + mac(2 * dim, slots, rows),
        moved=dim * nrel * 8,
        collective_id=1,
        has_side_effects=True,
    )(target_grad, targets, coef, sources, weights, src, rid, asked, ent_t, as_row(entity_state))
    new_rel, rel_after = call(
        functools.partial(relation_kernel, share, pieces),
        [((dim, nrel), f32), ((1, nrel), f32)],
        moved=dim * nrel * 10,
    )(*codes, rel_t, as_row(relation_state))
    return (
        new_ent.T,
        ent_after.reshape(rows),
        new_rel.T,
        rel_after.reshape(nrel),
        edge_loss.reshape(edges),
    )


def solution(mesh):
    placed = (
        P(("groups", "ent"), None),
        P(("groups", "ent")),
        P("groups", None),
        P("groups"),
        P(("groups", "ent")),
        P(("groups", "ent"), None),
        P(("groups", "ent")),
        P(("groups", "ent")),
    )
    return jax.shard_map(
        on_device,
        mesh=mesh,
        in_specs=placed,
        out_specs=(
            P(("groups", "ent"), None),
            P(("groups", "ent")),
            P("groups", None),
            P("groups"),
            P(("groups", "ent")),
        ),
        check_vma=False,
    )
```
